256 devices in a mesh: segment: 2 (over core), tile: 8 (over x_lo, y), chan: 16 (over z, x_hi).
Axes of the slice: x: 4 (x_hi: 2, x_lo: 2; x = x_hi * 2 + x_lo), y: 4, z: 8, core: 2. Of those that a mesh axis runs over, the one named last changes fastest.
Arguments:
- video: bfloat16 [2, 16, 128, 256, 256], P('segment', None, ('tile', 'chan')), may hold values from -6 to 6
- spatial_weight: bfloat16 [9, 256, 256], replicated, may hold values from -0.125 to 0.125
- temporal_weight: bfloat16 [3, 256, 512], replicated, may hold values from -0.21875 to 0.21875
- latent_grad: bfloat16 [2, 8, 128, 256, 512], P('segment', 'tile', None, 'chan'), may hold values from -0.008239746 to 0.008239746
Outputs:
- latents: bfloat16 [2, 8, 128, 256, 512], P('segment', 'tile', None, 'chan')
- temporal_grad: float32 [3, 256, 512], replicated
The draws below stay inside these ranges and needn't reach their ends.
All inputs are finite; a program needn't handle non-finite values.
Results may differ from the reference program's by a relative error of at most 0.005.
Values may be sent and summed in bfloat16 or wider, within the bound.
No kernel may reach another device: no remote copies, remote signals or barrier semaphores. Data moves between devices by JAX's collectives and lax.ppermute only.
A program may use at most 128 MiB of HBM per device.

```python
import jax
import jax.numpy as jnp
from jax import lax

C = 256
C2 = 512
F = 16
ROWS = 128
W = 256


def shard_levels(rng, shape, shards, low, top_value):
    def one(dim, blocks):
        steps = jax.random.uniform(jax.random.fold_in(jax.random.fold_in(rng, 6), dim), (blocks,), jnp.float32, low / len(shards), top_value / len(shards))
        return jnp.repeat(jnp.exp(steps), shape[dim] // blocks).reshape((-1,) + (1,) * (len(shape) - dim - 1))

    factor_of = one(*shards[0])
    for cut in shards[1:]:
        factor_of = factor_of * one(*cut)
    return factor_of


def normal_values(own_key, extent, spread, bound, split=(), held_as=jnp.bfloat16):
    loudness = shard_levels(own_key, extent, split, -0.22, 0.18) if split else 1.0
    entries = jax.random.normal(own_key, extent, jnp.float32) * spread * loudness
    return jnp.minimum(jnp.maximum(entries, -bound), bound).astype(held_as)


def setup_inputs(seed: int = 0) -> dict:
    key_of = jax.random.split(jax.random.key(seed), 5)
    video = normal_values(key_of[0], (2, F, ROWS, W, C), 1.0, 6.0, ((0, 2), (2, 128)))
    spatial_weight = normal_values(key_of[1], (9, C, C), (9 * C) ** -0.5, 0.125)
    temporal_weight = normal_values(key_of[2], (3, C, C2), (3 * C) ** -0.5, 0.21875)
    latent_grad = normal_values(key_of[3], (2, F // 2, ROWS, W, C2), ((F * ROWS * W) ** -0.5), 0.008239746, ((0, 2), (1, 8), (3, 16)))
    return {"video": video, "spatial_weight": spatial_weight, "temporal_weight": temporal_weight, "latent_grad": latent_grad}


def spatial_conv(frame, spatial_weight):
    padded = jnp.pad(frame, ((1, 1), (1, 1), (0, 0)))
    total = jnp.zeros((ROWS * W, C), jnp.float32)
    for across in range(3):
        for along in range(3):
            window = padded[across:across + ROWS, along:along + W].reshape((-1, C))
            total = total + jnp.dot(window, spatial_weight[3 * across + along], preferred_element_type=jnp.float32)
    return jax.nn.silu(total).astype(jnp.bfloat16).reshape((ROWS, W, C))


def reference(video, spatial_weight, temporal_weight, latent_grad):
    frames = video.reshape((2 * F, ROWS, W, C))
    activated = lax.map(lambda frame: spatial_conv(frame, spatial_weight), frames).reshape((2, F, ROWS, W, C))
    upstream_all = latent_grad[::-1]

    def step(total, index):
        upstream = lax.dynamic_index_in_dim(upstream_all, index, 1, keepdims=False).reshape((-1, C2))
        latent = jnp.zeros((2 * ROWS * W, C2), jnp.float32)
        for offset in range(3):
            wanted = (2 * index - 2 + offset).astype(jnp.int32)
            picked = lax.dynamic_index_in_dim(activated, jnp.maximum(wanted, 0).astype(jnp.int32), 1, keepdims=False)
            valid = (wanted >= 0).astype(jnp.bfloat16)
            flat = (picked * valid).reshape((-1, C))
            latent = latent + jnp.dot(flat, temporal_weight[offset], preferred_element_type=jnp.float32)
            term = lax.dot_general(flat, upstream, (((0,), (0,)), ((), ())), preferred_element_type=jnp.float32)
            total = total.at[offset].add(term)
        return total, latent.astype(jnp.bfloat16).reshape((2, ROWS, W, C2))

    grad, latents = lax.scan(step, jnp.zeros((3, C, C2), jnp.float32), jnp.arange(F // 2, dtype=jnp.int32))
    return jnp.moveaxis(latents, 0, 1), grad
```

```python
import jax
import jax.numpy as jnp
from jax import lax
from jax.sharding import PartitionSpec as P

GROUP = ("tile", "chan")


def exchange(pieces):
    return lax.all_to_all(pieces, GROUP, split_axis=0, concat_axis=0, tiled=True)


def other_core(shard):
    return lax.ppermute(shard, "segment", [(0, 1), (1, 0)])


def column_windows(frames, chans):
    num, width, channels = frames.shape
    blocks = frames.reshape((num, chans, width // chans, channels))
    blank = jnp.zeros((num, 1, 1, channels), frames.dtype)
    left = jnp.concatenate([blank, blocks[:, :-1, -1:]], axis=1)
    right = jnp.concatenate([blocks[:, 1:, :1], blank], axis=1)
    return jnp.concatenate([left, blocks, right], axis=2)


def activate(columns, spatial_weight):
    channels = columns.shape[2]
    pre = lax.conv_general_dilated(
        columns[None],
        spatial_weight.reshape((3, 3, channels, channels)),
        (1, 1),
        ((1, 1), (0, 0)),
        dimension_numbers=("NHWC", "HWIO", "NHWC"),
        preferred_element_type=jnp.float32,
    )
    return jax.nn.silu(pre).astype(jnp.bfloat16).reshape((-1, channels))


def contract_rows(flat, upstream):
    return lax.dot_general(
        flat, upstream, (((0,), (0,)), ((), ())), preferred_element_type=jnp.float32
    )


def summed(partial, devices):
    side = lax.axis_index("segment")
    flat = partial.reshape((2, devices, -1, 128))
    mine = lax.dynamic_index_in_dim(flat, side, 0, keepdims=False)
    sent = lax.dynamic_index_in_dim(flat, 1 - side, 0, keepdims=False)
    pair = mine + other_core(sent)
    piece = jnp.sum(exchange(pair), axis=0).astype(jnp.bfloat16)
    whole = exchange(jnp.broadcast_to(piece[None], (devices, *piece.shape)))
    away = other_core(whole)
    low = jnp.where(side == 0, whole, away)
    high = jnp.where(side == 0, away, whole)
    return jnp.stack([low, high]).astype(jnp.float32).reshape(partial.shape)


def body(video, spatial_weight, temporal_weight, latent_grad):
    tiles, chans = lax.axis_size("tile"), lax.axis_size("chan")
    devices = tiles * chans
    frames = video[0, :, 0]
    channels = frames.shape[2]
    upstream = other_core(latent_grad)
    flat_up = upstream.reshape((-1, upstream.shape[4]))
    windows = column_windows(frames, chans)
    even = windows[0::2].reshape((devices, -1, channels))
    odd = jnp.concatenate([windows[-1:], windows[1:-1:2]]).reshape((devices, -1, channels))
    even_cols = exchange(even)
    odd_cols = exchange(odd)
    newest = activate(even_cols, spatial_weight)
    oldest = lax.ppermute(newest, "tile", [(i, i + 1) for i in range(tiles - 1)])
    middle = activate(odd_cols, spatial_weight)
    middle = jnp.where(lax.axis_index("tile") > 0, middle, jnp.zeros_like(middle))
    taps = (oldest, middle, newest)
    latent = sum(
        jnp.dot(tap, temporal_weight[k], preferred_element_type=jnp.float32)
        for k, tap in enumerate(taps)
    )
    latents = latent.astype(jnp.bfloat16).reshape(upstream.shape)
    partial = jnp.stack([contract_rows(tap, flat_up) for tap in taps])
    return (latents, summed(partial, devices))


def solution(mesh):
    placed = (
        P("segment", None, ("tile", "chan"), None, None),
        P(),
        P(),
        P("segment", "tile", None, "chan", None),
    )
    return jax.shard_map(
        body,
        mesh=mesh,
        in_specs=placed,
        out_specs=(P("segment", "tile", None, "chan", None), P()),
        check_vma=False,
    )
```

```python
import functools

import jax
import jax.numpy as jnp
from jax import lax
from jax.experimental import pallas as pl
from jax.experimental.pallas import tpu as pltpu
from jax.sharding import PartitionSpec as P

GROUP = ("tile", "chan")
LANES = 128
COLS = 16
PIECE = 16
VMEM_BYTES = 48 * 1024 * 1024
F32 = jnp.float32
BF16 = jnp.bfloat16


def exchange(pieces):
    return lax.all_to_all(pieces, GROUP, split_axis=0, concat_axis=0, tiled=True)


def other_core(shard):
    return lax.ppermute(shard, "segment", [(0, 1), (1, 0)])


def pack_kernel(odd_ref, even_ref, out_ref):
    frames = (odd_ref[0], even_ref[0])
    blocks, height = out_ref.shape[0], out_ref.shape[1]
    place = lax.broadcasted_iota(jnp.int32, (blocks, 8, LANES), 1)
    edges = jnp.zeros((blocks, 8, LANES), F32)
    for f, frame in enumerate(frames):
        for h in range(2):
            half = frame[:, h * LANES : (h + 1) * LANES].reshape((blocks, COLS, LANES))
            start = h * 2 * COLS + f * COLS
            out_ref[:, start : start + COLS, :] = half
            wide = half.astype(F32)
            blank = jnp.zeros((1, 1, LANES), F32)
            left = jnp.concatenate([blank, wide[:-1, COLS - 1 :]], axis=0)
            right = jnp.concatenate([wide[1:, :1], blank], axis=0)
            row = h * 4 + f * 2
            edges = jnp.where(place == row, left, edges)
            edges = jnp.where(place == row + 1, right, edges)
    out_ref[:, height - 8 :, :] = edges.astype(BF16)


def pack(frames, tiles, chans):
    num, width, channels = frames.shape
    height = 4 * COLS + 8
    return pl.pallas_call(
        pack_kernel,
        grid=(tiles,),
        in_specs=[
            pl.BlockSpec((1, width, channels), lambda j: ((2 * j + num - 1) % num, 0, 0)),
            pl.BlockSpec((1, width, channels), lambda j: (2 * j, 0, 0)),
        ],
        out_specs=pl.BlockSpec((chans, height, LANES), lambda j: (j, 0, 0)),
        out_shape=jax.ShapeDtypeStruct((tiles * chans, height, LANES), BF16),
        compiler_params=pltpu.CompilerParams(vmem_limit_bytes=VMEM_BYTES),
        name="pack",
    )(frames, frames)


def silu(pre):
    return pre / (1.0 + jnp.exp(-pre))


def conv_kernel(
    rows, chunk, where_ref, y_hbm, w_hbm, u_hbm, next_hbm,
    act_ref, mine_ref, sent_ref, y_ref, w_ref, u_ref, next_ref, window_ref, grad_ref, sems,
):
    copies = [
        pltpu.make_async_copy(src, dst, sems.at[i])
        for i, (src, dst) in enumerate(
            ((y_hbm, y_ref), (w_hbm, w_ref), (u_hbm, u_ref), (next_hbm, next_ref))
        )
    ]
    for copy in copies:
        copy.start()
    channels = 2 * LANES
    side, tile = where_ref[0], where_ref[1]
    window_ref[0] = jnp.zeros(window_ref.shape[1:], BF16)
    window_ref[rows + 1] = jnp.zeros(window_ref.shape[1:], BF16)
    copies[0].wait()
    for f in (1, 0):
        for r in range(0, rows, chunk):
            place = lax.broadcasted_iota(jnp.int32, (chunk, COLS, LANES), 1)
            edges = y_ref[r : r + chunk, 4 * COLS :, :].astype(F32)
            for h in range(2):
                start = h * 2 * COLS + f * COLS
                main = y_ref[r : r + chunk, start : start + COLS, :]
                wide = main.astype(F32).reshape((chunk * COLS, LANES))
                row = h * 4 + f * 2
                shape = (chunk, COLS, LANES)
                earlier = pltpu.roll(wide, 1, 0).reshape(shape)
                later = pltpu.roll(wide, chunk * COLS - 1, 0).reshape(shape)
                earlier = jnp.where(place == 0, edges[:, row : row + 1], earlier)
                later = jnp.where(place == COLS - 1, edges[:, row + 1 : row + 2], later)
                for e, part in enumerate((earlier.astype(BF16), main, later.astype(BF16))):
                    lane = e * channels + h * LANES
                    window_ref[r + 1 : r + 1 + chunk, :, lane : lane + LANES] = part
        if f == 1:
            copies[1].wait()
        for r in range(0, rows, chunk):
            pre = jnp.zeros((chunk * COLS, channels), F32)
            for a in range(3):
                lhs = window_ref[r + a : r + a + chunk].reshape((chunk * COLS, 3 * channels))
                pre = pre + jnp.dot(lhs, w_ref[a], preferred_element_type=F32)
            value = silu(pre)
            if f == 0:
                value = jnp.where(tile > 0, value, jnp.zeros_like(value))
            act_ref[f, r * COLS : (r + chunk) * COLS, :] = value.astype(BF16)
    copies[2].wait()
    copies[3].wait()
    lanes = grad_ref.shape[1]
    blocks = u_ref.shape[1] // LANES
    for k, (f, up) in enumerate(((1, next_ref), (0, u_ref), (1, u_ref))):
        term = lax.dot_general(
            act_ref[f], up[...], (((0,), (0,)), ((), ())), preferred_element_type=F32
        )
        for g in range(channels // PIECE):
            line = k * channels + g * PIECE
            half, group = divmod(line, 3 * channels // 2)
            for b in range(blocks):
                grad_ref[half, (group // PIECE) * blocks + b] = term[
                    g * PIECE : (g + 1) * PIECE, b * LANES : (b + 1) * LANES
                ]
    mine_ref[...] = grad_ref[side]
    sent_ref[...] = grad_ref[1 - side]


def conv_and_gradient(where, pieces, spatial_weight, upstream, following):
    rows = pieces.shape[0]
    channels = spatial_weight.shape[2]
    out_channels = upstream.shape[1]
    positions = rows * COLS
    count = 3 * channels * out_channels // (2 * PIECE * LANES)
    hbm = pl.BlockSpec(memory_space=pl.ANY)
    vmem = pl.BlockSpec(memory_space=pltpu.VMEM)
    weight = spatial_weight.reshape((3, 3 * channels, channels))
    part = jax.ShapeDtypeStruct((count, PIECE, LANES), F32)
    return pl.pallas_call(
        functools.partial(conv_kernel, rows, 32),
        in_specs=[pl.BlockSpec(memory_space=pltpu.SMEM), hbm, hbm, hbm, hbm],
        out_specs=[vmem, vmem, vmem],
        out_shape=[jax.ShapeDtypeStruct((2, positions, channels), BF16), part, part],
        scratch_shapes=[
            pltpu.VMEM(pieces.shape, BF16),
            pltpu.VMEM(weight.shape, BF16),
            pltpu.VMEM(upstream.shape, BF16),
            pltpu.VMEM(following.shape, BF16),
            pltpu.VMEM((rows + 2, COLS, 3 * channels), BF16),
            pltpu.VMEM((2, count, PIECE, LANES), F32),
            pltpu.SemaphoreType.DMA((4,)),
        ],
        compiler_params=pltpu.CompilerParams(vmem_limit_bytes=VMEM_BYTES),
        cost_estimate=pl.CostEstimate(
            flops=2 * positions * (18 * channels * channels + 3 * channels * out_channels),
            bytes_accessed=10_000_000,
            transcendentals=2 * positions * channels,
        ),
        name="conv_and_gradient",
    )(where, pieces, weight, upstream, following)


def latent_kernel(old_ref, act_ref, weight_ref, out_ref):
    total = jnp.dot(old_ref[...], weight_ref[0], preferred_element_type=F32)
    total = total + jnp.dot(act_ref[0], weight_ref[1], preferred_element_type=F32)
    total = total + jnp.dot(act_ref[1], weight_ref[2], preferred_element_type=F32)
    out_ref[...] = total.astype(BF16)


def temporal(oldest, acts, temporal_weight):
    positions, channels = oldest.shape
    out_channels = temporal_weight.shape[2]
    step = 512
    return pl.pallas_call(
        latent_kernel,
        grid=(positions // step,),
        in_specs=[
            pl.BlockSpec((step, channels), lambda i: (i, 0)),
            pl.BlockSpec((2, step, channels), lambda i: (0, i, 0)),
            pl.BlockSpec(temporal_weight.shape, lambda i: (0, 0, 0)),
        ],
        out_specs=pl.BlockSpec((step, out_channels), lambda i: (i, 0)),
        out_shape=jax.ShapeDtypeStruct((positions, out_channels), BF16),
        compiler_params=pltpu.CompilerParams(vmem_limit_bytes=VMEM_BYTES),
        cost_estimate=pl.CostEstimate(
            flops=6 * positions * channels * out_channels,
            bytes_accessed=6_000_000,
            transcendentals=0,
        ),
        name="temporal",
    )(oldest, acts, temporal_weight)


def total_kernel(parts_ref, after_ref, out_ref):
    total = jnp.sum(parts_ref[...].astype(F32), axis=0).astype(BF16)
    out_ref[...] = jnp.broadcast_to(total[None], out_ref.shape)


def total_for_all(parts, after):
    vmem = pl.BlockSpec(memory_space=pltpu.VMEM)
    return pl.pallas_call(
        total_kernel,
        in_specs=[vmem, pl.BlockSpec(memory_space=pl.ANY)],
        out_specs=vmem,
        out_shape=jax.ShapeDtypeStruct(parts.shape, BF16),
        compiler_params=pltpu.CompilerParams(vmem_limit_bytes=VMEM_BYTES),
        name="total_for_all",
    )(parts, after)


def unpack_kernel(where_ref, own_ref, away_ref, out_ref):
    side = where_ref[0]
    blocks = out_ref.shape[2] // LANES
    for ref, half in ((own_ref, side), (away_ref, 1 - side)):
        for p in range(away_ref.shape[0]):
            g, b = divmod(p, blocks)
            out_ref[half, g * PIECE : (g + 1) * PIECE, b * LANES : (b + 1) * LANES] = ref[p].astype(F32)


def unpack(where, own, away, height, width):
    vmem = pl.BlockSpec(memory_space=pltpu.VMEM)
    return pl.pallas_call(
        unpack_kernel,
        in_specs=[pl.BlockSpec(memory_space=pltpu.SMEM), vmem, vmem],
        out_specs=vmem,
        out_shape=jax.ShapeDtypeStruct((2, height // 2, width), F32),
        compiler_params=pltpu.CompilerParams(vmem_limit_bytes=VMEM_BYTES),
        name="unpack",
    )(where, own, away)


def body(video, spatial_weight, temporal_weight, latent_grad):
    tiles, chans = lax.axis_size("tile"), lax.axis_size("chan")
    devices = tiles * chans
    where = jnp.stack([lax.axis_index("segment"), lax.axis_index("tile")]).astype(jnp.int32)
    out_channels = latent_grad.shape[4]
    upstream = other_core(latent_grad)
    shift = [
        (s * tiles + j, (1 - s) * tiles + j - 1) for s in range(2) for j in range(1, tiles)
    ]
    following = lax.ppermute(latent_grad, ("segment", "tile"), shift)
    pieces = exchange(pack(video[0, :, 0], tiles, chans))
    acts, mine, sent = conv_and_gradient(
        where,
        pieces,
        spatial_weight,
        upstream.reshape((-1, out_channels)),
        following.reshape((-1, out_channels)),
    )
    oldest = lax.ppermute(acts[1], "tile", [(i, i + 1) for i in range(tiles - 1)])
    pair = (mine + other_core(sent)).astype(BF16)
    count = pair.shape[0]
    pair = jnp.pad(pair, ((0, devices - count), (0, 0), (0, 0)))
    whole = exchange(total_for_all(exchange(pair), oldest))[:count]
    grad = unpack(where, whole, other_core(whole), temporal_weight.shape[0] * temporal_weight.shape[1], out_channels)
    latents = temporal(oldest, acts, temporal_weight).reshape(upstream.shape)
    return (latents, grad.reshape(temporal_weight.shape))


def solution(mesh):
    placed = (
        P("segment", None, ("tile", "chan"), None, None),
        P(),
        P(),
        P("segment", "tile", None, "chan", None),
    )
    return jax.shard_map(
        body,
        mesh=mesh,
        in_specs=placed,
        out_specs=(P("segment", "tile", None, "chan", None), P()),
        check_vma=False,
    )
```

```python
import functools

import jax
import jax.numpy as jnp
from jax import lax
from jax.experimental import pallas as pl
from jax.experimental.pallas import tpu as pltpu
from jax.sharding import PartitionSpec as P

GROUP = ("tile", "chan")
LANES = 128
COLS = 16
PIECE = 16
VMEM_BYTES = 32 * 1024 * 1024
F32 = jnp.float32
BF16 = jnp.bfloat16


def exchange(pieces):
    return lax.all_to_all(pieces, GROUP, split_axis=0, concat_axis=0, tiled=True)


def other_core(shard):
    return lax.ppermute(shard, "segment", [(0, 1), (1, 0)])


def pack_kernel(odd_ref, even_ref, out_ref):
    frames = (odd_ref[0], even_ref[0])
    blocks, height = out_ref.shape[0], out_ref.shape[1]
    place = lax.broadcasted_iota(jnp.int32, (blocks, 8, LANES), 1)
    edges = jnp.zeros((blocks, 8, LANES), F32)
    for f, frame in enumerate(frames):
        for h in range(2):
            half = frame[:, h * LANES : (h + 1) * LANES].reshape((blocks, COLS, LANES))
            start = h * 2 * COLS + f * COLS
            out_ref[:, start : start + COLS, :] = half
            wide = half.astype(F32)
            blank = jnp.zeros((1, 1, LANES), F32)
            left = jnp.concatenate([blank, wide[:-1, COLS - 1 :]], axis=0)
            right = jnp.concatenate([wide[1:, :1], blank], axis=0)
            row = h * 4 + f * 2
            edges = jnp.where(place == row, left, edges)
            edges = jnp.where(place == row + 1, right, edges)
    out_ref[:, height - 8 :, :] = edges.astype(BF16)


def pack(frames, tiles, chans):
    num, width, channels = frames.shape
    height = 4 * COLS + 8
    return pl.pallas_call(
        pack_kernel,
        grid=(tiles,),
        in_specs=[
            pl.BlockSpec((1, width, channels), lambda j: ((2 * j + num - 1) % num, 0, 0)),
            pl.BlockSpec((1, width, channels), lambda j: (2 * j, 0, 0)),
        ],
        out_specs=pl.BlockSpec((chans, height, LANES), lambda j: (j, 0, 0)),
        out_shape=jax.ShapeDtypeStruct((tiles * chans, height, LANES), BF16),
        compiler_params=pltpu.CompilerParams(vmem_limit_bytes=VMEM_BYTES),
        name="pack",
    )(frames, frames)


def silu(pre):
    return pre / (1.0 + jnp.exp(-pre))


def conv_kernel(
    rows, chunk, where_ref, y_hbm, w_hbm, odd_ref, even_ref, y_ref, w_ref, window_ref, y_sems, w_sem
):
    channels = 2 * LANES
    loads = []
    for i, r in enumerate(range(0, rows, chunk)):
        part = pl.ds(r, chunk)
        loads.append(pltpu.make_async_copy(y_hbm.at[part], y_ref.at[part], y_sems.at[i]))
    weights = pltpu.make_async_copy(w_hbm, w_ref, w_sem)
    for load in loads:
        load.start()
    weights.start()
    tile = where_ref[1]
    window_ref[0] = jnp.zeros(window_ref.shape[1:], BF16)
    window_ref[rows + 1] = jnp.zeros(window_ref.shape[1:], BF16)
    for f, act_ref in ((1, even_ref), (0, odd_ref)):
        for r in range(0, rows, chunk):
            if f == 1:
                loads[r // chunk].wait()
            place = lax.broadcasted_iota(jnp.int32, (chunk, COLS, LANES), 1)
            edges = y_ref[r : r + chunk, 4 * COLS :, :].astype(F32)
            for h in range(2):
                start = h * 2 * COLS + f * COLS
                main = y_ref[r : r + chunk, start : start + COLS, :]
                wide = main.astype(F32).reshape((chunk * COLS, LANES))
                row = h * 4 + f * 2
                shape = (chunk, COLS, LANES)
                earlier = pltpu.roll(wide, 1, 0).reshape(shape)
                later = pltpu.roll(wide, chunk * COLS - 1, 0).reshape(shape)
                earlier = jnp.where(place == 0, edges[:, row : row + 1], earlier)
                later = jnp.where(place == COLS - 1, edges[:, row + 1 : row + 2], later)
                for e, part in enumerate((earlier.astype(BF16), main, later.astype(BF16))):
                    lane = e * channels + h * LANES
                    window_ref[r + 1 : r + 1 + chunk, :, lane : lane + LANES] = part
        if f == 1:
            weights.wait()
        for r in range(0, rows, chunk):
            pre = jnp.zeros((chunk * COLS, channels), F32)
            for a in range(3):
                lhs = window_ref[r + a : r + a + chunk].reshape((chunk * COLS, 3 * channels))
                pre = pre + jnp.dot(lhs, w_ref[a], preferred_element_type=F32)
            value = silu(pre)
            if f == 0:
                value = jnp.where(tile > 0, value, jnp.zeros_like(value))
            act_ref[r * COLS : (r + chunk) * COLS, :] = value.astype(BF16)


def spatial(where, pieces, spatial_weight):
    rows = pieces.shape[0]
    channels = spatial_weight.shape[2]
    positions = rows * COLS
    chunk = 32
    weight = spatial_weight.reshape((3, 3 * channels, channels))
    hbm = pl.BlockSpec(memory_space=pltpu.HBM)
    vmem = pl.BlockSpec(memory_space=pltpu.VMEM)
    act = jax.ShapeDtypeStruct((positions, channels), BF16)
    return pl.pallas_call(
        functools.partial(conv_kernel, rows, chunk),
        in_specs=[pl.BlockSpec(memory_space=pltpu.SMEM), hbm, hbm],
        out_specs=[vmem, vmem],
        out_shape=[act, act],
        scratch_shapes=[
            pltpu.VMEM(pieces.shape, BF16),
            pltpu.VMEM(weight.shape, BF16),
            pltpu.VMEM((rows + 2, COLS, 3 * channels), BF16),
            pltpu.SemaphoreType.DMA((rows // chunk,)),
            pltpu.SemaphoreType.DMA,
        ],
        compiler_params=pltpu.CompilerParams(vmem_limit_bytes=VMEM_BYTES),
        cost_estimate=pl.CostEstimate(
            flops=36 * positions * channels * channels,
            bytes_accessed=6_000_000,
            transcendentals=2 * positions * channels,
        ),
        name="spatial",
    )(where, pieces, weight)


def gradient_kernel(
    where_ref, odd_ref, even_ref, u_hbm, next_hbm, mine_ref, sent_ref, u_ref, next_ref, grad_ref, sems
):
    loads = (
        pltpu.make_async_copy(u_hbm, u_ref, sems.at[0]),
        pltpu.make_async_copy(next_hbm, next_ref, sems.at[1]),
    )
    for load in loads:
        load.start()
    side = where_ref[0]
    channels = odd_ref.shape[1]
    blocks = u_ref.shape[1] // LANES
    loads[0].wait()
    for k, act_ref, up in ((1, odd_ref, u_ref), (2, even_ref, u_ref), (0, even_ref, next_ref)):
        if k == 0:
            loads[1].wait()
        term = lax.dot_general(
            act_ref[...], up[...], (((0,), (0,)), ((), ())), preferred_element_type=F32
        )
        for g in range(channels // PIECE):
            line = k * channels + g * PIECE
            half, group = divmod(line, 3 * channels // 2)
            for b in range(blocks):
                grad_ref[half, (group // PIECE) * blocks + b] = term[
                    g * PIECE : (g + 1) * PIECE, b * LANES : (b + 1) * LANES
                ]
    mine_ref[...] = grad_ref[side]
    sent_ref[...] = grad_ref[1 - side]


def gradient(where, odd, even, upstream, following):
    positions, channels = odd.shape
    out_channels = upstream.shape[1]
    count = 3 * channels * out_channels // (2 * PIECE * LANES)
    vmem = pl.BlockSpec(memory_space=pltpu.VMEM)
    hbm = pl.BlockSpec(memory_space=pltpu.HBM)
    part = jax.ShapeDtypeStruct((count, PIECE, LANES), F32)
    return pl.pallas_call(
        gradient_kernel,
        in_specs=[pl.BlockSpec(memory_space=pltpu.SMEM), vmem, vmem, hbm, hbm],
        out_specs=[vmem, vmem],
        out_shape=[part, part],
        scratch_shapes=[
            pltpu.VMEM(upstream.shape, BF16),
            pltpu.VMEM(following.shape, BF16),
            pltpu.VMEM((2, count, PIECE, LANES), F32),
            pltpu.SemaphoreType.DMA((2,)),
        ],
        compiler_params=pltpu.CompilerParams(vmem_limit_bytes=VMEM_BYTES),
        cost_estimate=pl.CostEstimate(
            flops=6 * positions * channels * out_channels,
            bytes_accessed=8_000_000,
            transcendentals=0,
        ),
        name="gradient",
    )(where, odd, even, upstream, following)


def latent_kernel(old_ref, odd_ref, even_ref, weight_ref, out_ref):
    total = jnp.dot(old_ref[...], weight_ref[0], preferred_element_type=F32)
    total = total + jnp.dot(odd_ref[...], weight_ref[1], preferred_element_type=F32)
    total = total + jnp.dot(even_ref[...], weight_ref[2], preferred_element_type=F32)
    out_ref[...] = total.astype(BF16)


def temporal(oldest, odd, even, temporal_weight):
    positions, channels = oldest.shape
    out_channels = temporal_weight.shape[2]
    step = 512
    tap = pl.BlockSpec((step, channels), lambda i: (i, 0))
    return pl.pallas_call(
        latent_kernel,
        grid=(positions // step,),
        in_specs=[
            tap,
            tap,
            tap,
            pl.BlockSpec(temporal_weight.shape, lambda i: (0, 0, 0)),
        ],
        out_specs=pl.BlockSpec((step, out_channels), lambda i: (i, 0)),
        out_shape=jax.ShapeDtypeStruct((positions, out_channels), BF16),
        compiler_params=pltpu.CompilerParams(vmem_limit_bytes=VMEM_BYTES),
        cost_estimate=pl.CostEstimate(
            flops=6 * positions * channels * out_channels,
            bytes_accessed=6_000_000,
            transcendentals=0,
        ),
        name="temporal",
    )(oldest, odd, even, temporal_weight)


def total_kernel(parts_ref, out_ref):
    total = jnp.sum(parts_ref[...].astype(F32), axis=0).astype(BF16)
    out_ref[...] = jnp.broadcast_to(total[None], out_ref.shape)


def total_for_all(parts):
    vmem = pl.BlockSpec(memory_space=pltpu.VMEM)
    return pl.pallas_call(
        total_kernel,
        in_specs=[vmem],
        out_specs=vmem,
        out_shape=jax.ShapeDtypeStruct(parts.shape, BF16),
        compiler_params=pltpu.CompilerParams(vmem_limit_bytes=VMEM_BYTES),
        name="total_for_all",
    )(parts)


def unpack_kernel(where_ref, own_ref, away_ref, out_ref):
    side = where_ref[0]
    blocks = out_ref.shape[2] // LANES
    for ref, half in ((own_ref, side), (away_ref, 1 - side)):
        for p in range(away_ref.shape[0]):
            g, b = divmod(p, blocks)
            out_ref[half, g * PIECE : (g + 1) * PIECE, b * LANES : (b + 1) * LANES] = ref[p].astype(F32)


def unpack(where, own, away, height, width):
    vmem = pl.BlockSpec(memory_space=pltpu.VMEM)
    return pl.pallas_call(
        unpack_kernel,
        in_specs=[pl.BlockSpec(memory_space=pltpu.SMEM), vmem, vmem],
        out_specs=vmem,
        out_shape=jax.ShapeDtypeStruct((2, height // 2, width), F32),
        compiler_params=pltpu.CompilerParams(vmem_limit_bytes=VMEM_BYTES),
        name="unpack",
    )(where, own, away)


def body(video, spatial_weight, temporal_weight, latent_grad):
    tiles, chans = lax.axis_size("tile"), lax.axis_size("chan")
    devices = tiles * chans
    where = jnp.stack([lax.axis_index("segment"), lax.axis_index("tile")]).astype(jnp.int32)
    out_channels = latent_grad.shape[4]
    upstream = other_core(latent_grad)
    shift = [
        (s * tiles + j, (1 - s) * tiles + j - 1) for s in range(2) for j in range(1, tiles)
    ]
    following = lax.ppermute(latent_grad, ("segment", "tile"), shift)
    frames = pltpu.with_memory_space_constraint(video[0, :, 0], pltpu.HBM)
    pieces = pltpu.with_memory_space_constraint(exchange(pack(frames, tiles, chans)), pltpu.HBM)
    odd, even = spatial(where, pieces, spatial_weight)
    mine, sent = gradient(
        where,
        odd,
        even,
        upstream.reshape((-1, out_channels)),
        following.reshape((-1, out_channels)),
    )
    oldest = lax.ppermute(even, "tile", [(i, i + 1) for i in range(tiles - 1)])
    pair = (mine + other_core(sent)).astype(BF16)
    count = pair.shape[0]
    pair = jnp.pad(pair, ((0, devices - count), (0, 0), (0, 0)))
    whole = exchange(total_for_all(exchange(pair)))
    latents = temporal(oldest, odd, even, temporal_weight).reshape(upstream.shape)
    whole, latents = lax.optimization_barrier((whole, latents))
    whole = whole[:count]
    height = temporal_weight.shape[0] * temporal_weight.shape[1]
    grad = unpack(where, whole, other_core(whole), height, out_channels)
    return (latents, grad.reshape(temporal_weight.shape))


def solution(mesh):
    placed = (
        P("segment", None, ("tile", "chan"), None, None),
        P(),
        P(),
        P("segment", "tile", None, "chan", None),
    )
    return jax.shard_map(
        body,
        mesh=mesh,
        in_specs=placed,
        out_specs=(P("segment", "tile", None, "chan", None), P()),
        check_vma=False,
    )
```

```python
import functools

import jax
import jax.numpy as jnp
from jax import lax
from jax.experimental import pallas as pl
from jax.experimental.pallas import tpu as pltpu
from jax.sharding import PartitionSpec as P

GROUP = ("tile", "chan")
LANES = 128
COLS = 16
PIECE = 16
VMEM_BYTES = 32 * 1024 * 1024
F32 = jnp.float32
BF16 = jnp.bfloat16


def exchange(pieces):
    return lax.all_to_all(pieces, GROUP, split_axis=0, concat_axis=0, tiled=True)


def other_core(shard):
    return lax.ppermute(shard, "segment", [(0, 1), (1, 0)])


def pack_kernel(tiles, chans, frame_hbm, out_hbm, frame_ref, piece_ref, in_sems, out_sems):
    num = frame_hbm.shape[0]
    height = piece_ref.shape[1]
    loads = {}
    for j in range(tiles):
        for f in ((2 * j - 1) % num, 2 * j):
            loads[f] = pltpu.make_async_copy(frame_hbm.at[f], frame_ref.at[f], in_sems.at[f])
            loads[f].start()
    stores = []
    place = lax.broadcasted_iota(jnp.int32, (chans, 8, LANES), 1)
    blank = jnp.zeros((1, 1, LANES), F32)
    for j in range(tiles):
        edges = jnp.zeros((chans, 8, LANES), F32)
        block = pl.ds(j * chans, chans)
        for f, source in enumerate(((2 * j - 1) % num, 2 * j)):
            loads[source].wait()
            for h in range(2):
                half = frame_ref[source, :, h * LANES : (h + 1) * LANES]
                half = half.reshape((chans, COLS, LANES))
                start = h * 2 * COLS + f * COLS
                piece_ref[block, start : start + COLS, :] = half
                wide = half.astype(F32)
                left = jnp.concatenate([blank, wide[:-1, COLS - 1 :]], axis=0)
                right = jnp.concatenate([wide[1:, :1], blank], axis=0)
                row = h * 4 + f * 2
                edges = jnp.where(place == row, left, edges)
                edges = jnp.where(place == row + 1, right, edges)
        piece_ref[block, height - 8 :, :] = edges.astype(BF16)
        stores.append(pltpu.make_async_copy(piece_ref.at[block], out_hbm.at[block], out_sems.at[j]))
        stores[-1].start()
    for store in stores:
        store.wait()


def pack(frames, tiles, chans):
    hbm = pl.BlockSpec(memory_space=pltpu.HBM)
    pieces = jax.ShapeDtypeStruct((tiles * chans, 4 * COLS + 8, LANES), BF16)
    return pl.pallas_call(
        functools.partial(pack_kernel, tiles, chans),
        in_specs=[hbm],
        out_specs=hbm,
        out_shape=pieces,
        scratch_shapes=[
            pltpu.VMEM(frames.shape, BF16),
            pltpu.VMEM(pieces.shape, BF16),
            pltpu.SemaphoreType.DMA((frames.shape[0],)),
            pltpu.SemaphoreType.DMA((tiles,)),
        ],
        compiler_params=pltpu.CompilerParams(vmem_limit_bytes=VMEM_BYTES),
        name="pack",
    )(frames)


def mask_kernel(where_ref, out_ref):
    tile = where_ref[1]
    out_ref[...] = jnp.where(tile > 0, jnp.ones(out_ref.shape, F32), jnp.zeros(out_ref.shape, F32))


def odd_mask(where, channels):
    return pl.pallas_call(
        mask_kernel,
        in_specs=[pl.BlockSpec(memory_space=pltpu.SMEM)],
        out_specs=pl.BlockSpec(memory_space=pltpu.VMEM),
        out_shape=jax.ShapeDtypeStruct((8, channels), F32),
        cost_estimate=pl.CostEstimate(flops=10**12, bytes_accessed=10**9, transcendentals=0),
        name="odd_mask",
    )(where)


def silu(pre):
    return pre / (1.0 + jnp.exp(-pre))


def conv_kernel(
    rows, chunk, mask_hbm, y_hbm, w_hbm, odd_ref, even_ref,
    mask_ref, y_ref, w_ref, window_ref, y_sems, w_sem, mask_sem,
):
    channels = 2 * LANES
    loads = []
    for i, r in enumerate(range(0, rows, chunk)):
        part = pl.ds(r, chunk)
        loads.append(pltpu.make_async_copy(y_hbm.at[part], y_ref.at[part], y_sems.at[i]))
    weights = pltpu.make_async_copy(w_hbm, w_ref, w_sem)
    for load in loads:
        load.start()
    weights.start()
    mask = pltpu.make_async_copy(mask_hbm, mask_ref, mask_sem)
    mask.start()
    window_ref[0] = jnp.zeros(window_ref.shape[1:], BF16)
    window_ref[rows + 1] = jnp.zeros(window_ref.shape[1:], BF16)
    for f, act_ref in ((1, even_ref), (0, odd_ref)):
        for r in range(0, rows, chunk):
            if f == 1:
                loads[r // chunk].wait()
            place = lax.broadcasted_iota(jnp.int32, (chunk, COLS, LANES), 1)
            edges = y_ref[r : r + chunk, 4 * COLS :, :].astype(F32)
            for h in range(2):
                start = h * 2 * COLS + f * COLS
                main = y_ref[r : r + chunk, start : start + COLS, :]
                wide = main.astype(F32).reshape((chunk * COLS, LANES))
                row = h * 4 + f * 2
                shape = (chunk, COLS, LANES)
                earlier = pltpu.roll(wide, 1, 0).reshape(shape)
                later = pltpu.roll(wide, chunk * COLS - 1, 0).reshape(shape)
                earlier = jnp.where(place == 0, edges[:, row : row + 1], earlier)
                later = jnp.where(place == COLS - 1, edges[:, row + 1 : row + 2], later)
                for e, part in enumerate((earlier.astype(BF16), main, later.astype(BF16))):
                    lane = e * channels + h * LANES
                    window_ref[r + 1 : r + 1 + chunk, :, lane : lane + LANES] = part
        if f == 1:
            weights.wait()
            mask.wait()
            keep = mask_ref[0:1, :] > 0
        for r in range(0, rows, chunk):
            pre = jnp.zeros((chunk * COLS, channels), F32)
            for a in range(3):
                lhs = window_ref[r + a : r + a + chunk].reshape((chunk * COLS, 3 * channels))
                pre = pre + jnp.dot(lhs, w_ref[a], preferred_element_type=F32)
            value = silu(pre)
            if f == 0:
                value = jnp.where(keep, value, jnp.zeros_like(value))
            act_ref[r * COLS : (r + chunk) * COLS, :] = value.astype(BF16)


def spatial(mask, pieces, spatial_weight):
    rows = pieces.shape[0]
    channels = spatial_weight.shape[2]
    positions = rows * COLS
    chunk = 32
    weight = spatial_weight.reshape((3, 3 * channels, channels))
    hbm = pl.BlockSpec(memory_space=pltpu.HBM)
    vmem = pl.BlockSpec(memory_space=pltpu.VMEM)
    act = jax.ShapeDtypeStruct((positions, channels), BF16)
    return pl.pallas_call(
        functools.partial(conv_kernel, rows, chunk),
        in_specs=[hbm, hbm, hbm],
        out_specs=[vmem, vmem],
        out_shape=[act, act],
        scratch_shapes=[
            pltpu.VMEM(mask.shape, F32),
            pltpu.VMEM(pieces.shape, BF16),
            pltpu.VMEM(weight.shape, BF16),
            pltpu.VMEM((rows + 2, COLS, 3 * channels), BF16),
            pltpu.SemaphoreType.DMA((rows // chunk,)),
            pltpu.SemaphoreType.DMA,
            pltpu.SemaphoreType.DMA,
        ],
        compiler_params=pltpu.CompilerParams(vmem_limit_bytes=VMEM_BYTES),
        cost_estimate=pl.CostEstimate(
            flops=36 * positions * channels * channels,
            bytes_accessed=6_000_000,
            transcendentals=2 * positions * channels,
        ),
        name="spatial",
    )(mask, pieces, weight)


def gradient_kernel(
    where_ref, odd_ref, even_ref, u_hbm, next_hbm, mine_ref, sent_ref, u_ref, next_ref, grad_ref, sems
):
    loads = (
        pltpu.make_async_copy(u_hbm, u_ref, sems.at[0]),
        pltpu.make_async_copy(next_hbm, next_ref, sems.at[1]),
    )
    for load in loads:
        load.start()
    side = where_ref[0]
    channels = odd_ref.shape[1]
    blocks = u_ref.shape[1] // LANES
    loads[0].wait()
    for k, act_ref, up in ((1, odd_ref, u_ref), (2, even_ref, u_ref), (0, even_ref, next_ref)):
        if k == 0:
            loads[1].wait()
        term = lax.dot_general(
            act_ref[...], up[...], (((0,), (0,)), ((), ())), preferred_element_type=F32
        )
        for g in range(channels // PIECE):
            line = k * channels + g * PIECE
            half, group = divmod(line, 3 * channels // 2)
            for b in range(blocks):
                grad_ref[half, (group // PIECE) * blocks + b] = term[
                    g * PIECE : (g + 1) * PIECE, b * LANES : (b + 1) * LANES
                ]
    mine_ref[...] = grad_ref[side]
    sent_ref[...] = grad_ref[1 - side]


def gradient(where, odd, even, upstream, following):
    positions, channels = odd.shape
    out_channels = upstream.shape[1]
    count = 3 * channels * out_channels // (2 * PIECE * LANES)
    vmem = pl.BlockSpec(memory_space=pltpu.VMEM)
    hbm = pl.BlockSpec(memory_space=pltpu.HBM)
    part = jax.ShapeDtypeStruct((count, PIECE, LANES), F32)
    return pl.pallas_call(
        gradient_kernel,
        in_specs=[pl.BlockSpec(memory_space=pltpu.SMEM), vmem, vmem, hbm, hbm],
        out_specs=[vmem, vmem],
        out_shape=[part, part],
        scratch_shapes=[
            pltpu.VMEM(upstream.shape, BF16),
            pltpu.VMEM(following.shape, BF16),
            pltpu.VMEM((2, count, PIECE, LANES), F32),
            pltpu.SemaphoreType.DMA((2,)),
        ],
        compiler_params=pltpu.CompilerParams(vmem_limit_bytes=VMEM_BYTES),
        cost_estimate=pl.CostEstimate(
            flops=6 * positions * channels * out_channels,
            bytes_accessed=8_000_000,
            transcendentals=0,
        ),
        name="gradient",
    )(where, odd, even, upstream, following)


def latent_kernel(old_ref, odd_ref, even_ref, weight_ref, out_ref):
    total = jnp.dot(old_ref[...], weight_ref[0], preferred_element_type=F32)
    total = total + jnp.dot(odd_ref[...], weight_ref[1], preferred_element_type=F32)
    total = total + jnp.dot(even_ref[...], weight_ref[2], preferred_element_type=F32)
    out_ref[...] = total.astype(BF16)


def temporal(oldest, odd, even, temporal_weight):
    positions, channels = oldest.shape
    out_channels = temporal_weight.shape[2]
    step = 512
    tap = pl.BlockSpec((step, channels), lambda i: (i, 0))
    return pl.pallas_call(
        latent_kernel,
        grid=(positions // step,),
        in_specs=[
            tap,
            tap,
            tap,
            pl.BlockSpec(temporal_weight.shape, lambda i: (0, 0, 0)),
        ],
        out_specs=pl.BlockSpec((step, out_channels), lambda i: (i, 0)),
        out_shape=jax.ShapeDtypeStruct((positions, out_channels), BF16),
        compiler_params=pltpu.CompilerParams(vmem_limit_bytes=VMEM_BYTES),
        cost_estimate=pl.CostEstimate(
            flops=6 * positions * channels * out_channels,
            bytes_accessed=6_000_000,
            transcendentals=0,
        ),
        name="temporal",
    )(oldest, odd, even, temporal_weight)


def pair_kernel(mine_ref, away_ref, out_ref):
    count = mine_ref.shape[0]
    out_ref[:count] = (mine_ref[...] + away_ref[...]).astype(BF16)
    out_ref[count:] = jnp.zeros((out_ref.shape[0] - count, *out_ref.shape[1:]), BF16)


def pair_sum(mine, away, devices):
    vmem = pl.BlockSpec(memory_space=pltpu.VMEM)
    return pl.pallas_call(
        pair_kernel,
        in_specs=[vmem, vmem],
        out_specs=vmem,
        out_shape=jax.ShapeDtypeStruct((devices, *mine.shape[1:]), BF16),
        compiler_params=pltpu.CompilerParams(vmem_limit_bytes=VMEM_BYTES),
        name="pair_sum",
    )(mine, away)


def total_kernel(parts_ref, out_ref):
    total = jnp.sum(parts_ref[...].astype(F32), axis=0).astype(BF16)
    out_ref[...] = jnp.broadcast_to(total[None], out_ref.shape)


def total_for_all(parts):
    vmem = pl.BlockSpec(memory_space=pltpu.VMEM)
    return pl.pallas_call(
        total_kernel,
        in_specs=[vmem],
        out_specs=vmem,
        out_shape=jax.ShapeDtypeStruct(parts.shape, BF16),
        compiler_params=pltpu.CompilerParams(vmem_limit_bytes=VMEM_BYTES),
        name="total_for_all",
    )(parts)


def unpack_kernel(where_ref, own_ref, away_ref, out_ref):
    side = where_ref[0]
    blocks = out_ref.shape[2] // LANES
    for ref, half in ((own_ref, side), (away_ref, 1 - side)):
        for p in range(out_ref.shape[1] // PIECE * blocks):
            g, b = divmod(p, blocks)
            out_ref[half, g * PIECE : (g + 1) * PIECE, b * LANES : (b + 1) * LANES] = ref[p].astype(F32)


def unpack(where, own, away, height, width):
    vmem = pl.BlockSpec(memory_space=pltpu.VMEM)
    return pl.pallas_call(
        unpack_kernel,
        in_specs=[pl.BlockSpec(memory_space=pltpu.SMEM), vmem, vmem],
        out_specs=vmem,
        out_shape=jax.ShapeDtypeStruct((2, height // 2, width), F32),
        compiler_params=pltpu.CompilerParams(vmem_limit_bytes=VMEM_BYTES),
        name="unpack",
    )(where, own, away)


def body(video, spatial_weight, temporal_weight, latent_grad):
    tiles, chans = lax.axis_size("tile"), lax.axis_size("chan")
    devices = tiles * chans
    where = jnp.stack([lax.axis_index("segment"), lax.axis_index("tile")]).astype(jnp.int32)
    out_channels = latent_grad.shape[4]
    upstream = other_core(latent_grad)
    shift = [
        (s * tiles + j, (1 - s) * tiles + j - 1) for s in range(2) for j in range(1, tiles)
    ]
    following = lax.ppermute(latent_grad, ("segment", "tile"), shift)
    frames = pltpu.with_memory_space_constraint(video[0, :, 0], pltpu.HBM)
    pieces = pltpu.with_memory_space_constraint(exchange(pack(frames, tiles, chans)), pltpu.HBM)
    mask = pltpu.with_memory_space_constraint(odd_mask(where, video.shape[4]), pltpu.HBM)
    odd, even = spatial(mask, pieces, spatial_weight)
    mine, sent = gradient(
        where,
        odd,
        even,
        upstream.reshape((-1, out_channels)),
        following.reshape((-1, out_channels)),
    )
    oldest = lax.ppermute(even, "tile", [(i, i + 1) for i in range(tiles - 1)])
    pair = pair_sum(mine, other_core(sent), devices)
    whole = exchange(total_for_all(exchange(pair)))
    latents = temporal(oldest, odd, even, temporal_weight).reshape(upstream.shape)
    whole, latents = lax.optimization_barrier((whole, latents))
    height = temporal_weight.shape[0] * temporal_weight.shape[1]
    grad = unpack(where, whole, other_core(whole), height, out_channels)
    return (latents, grad.reshape(temporal_weight.shape))


def solution(mesh):
    placed = (
        P("segment", None, ("tile", "chan"), None, None),
        P(),
        P(),
        P("segment", "tile", None, "chan", None),
    )
    return jax.shard_map(
        body,
        mesh=mesh,
        in_specs=placed,
        out_specs=(P("segment", "tile", None, "chan", None), P()),
        check_vma=False,
    )
```

```python
import functools

import jax
import jax.numpy as jnp
from jax import lax
from jax.experimental import pallas as pl
from jax.experimental.pallas import tpu as pltpu
from jax.sharding import PartitionSpec as P

GROUP = ("tile", "chan")
LANES = 128
COLS = 16
PIECE = 16
VMEM_BYTES = 32 * 1024 * 1024
F32 = jnp.float32
BF16 = jnp.bfloat16


def exchange(pieces):
    return lax.all_to_all(pieces, GROUP, split_axis=0, concat_axis=0, tiled=True)


def other_core(shard):
    return lax.ppermute(shard, "segment", [(0, 1), (1, 0)])


def pack_kernel(tiles, chans, frame_hbm, out_hbm, frame_ref, piece_ref, in_sems, out_sems):
    num = frame_hbm.shape[0]
    height = piece_ref.shape[1]
    loads = {}
    for j in range(tiles):
        for f in ((2 * j - 1) % num, 2 * j):
            loads[f] = pltpu.make_async_copy(frame_hbm.at[f], frame_ref.at[f], in_sems.at[f])
            loads[f].start()
    stores = []
    place = lax.broadcasted_iota(jnp.int32, (chans, 8, LANES), 1)
    blank = jnp.zeros((1, 1, LANES), F32)
    for j in range(tiles):
        edges = jnp.zeros((chans, 8, LANES), F32)
        block = pl.ds(j * chans, chans)
        for f, source in enumerate(((2 * j - 1) % num, 2 * j)):
            loads[source].wait()
            for h in range(2):
                half = frame_ref[source, :, h * LANES : (h + 1) * LANES]
                half = half.reshape((chans, COLS, LANES))
                start = h * 2 * COLS + f * COLS
                piece_ref[block, start : start + COLS, :] = half
                wide = half.astype(F32)
                left = jnp.concatenate([blank, wide[:-1, COLS - 1 :]], axis=0)
                right = jnp.concatenate([wide[1:, :1], blank], axis=0)
                row = h * 4 + f * 2
                edges = jnp.where(place == row, left, edges)
                edges = jnp.where(place == row + 1, right, edges)
        piece_ref[block, height - 8 :, :] = edges.astype(BF16)
        stores.append(pltpu.make_async_copy(piece_ref.at[block], out_hbm.at[block], out_sems.at[j]))
        stores[-1].start()
    for store in stores:
        store.wait()


def pack(frames, tiles, chans):
    hbm = pl.BlockSpec(memory_space=pltpu.HBM)
    pieces = jax.ShapeDtypeStruct((tiles * chans, 4 * COLS + 8, LANES), BF16)
    return pl.pallas_call(
        functools.partial(pack_kernel, tiles, chans),
        in_specs=[hbm],
        out_specs=hbm,
        out_shape=pieces,
        scratch_shapes=[
            pltpu.VMEM(frames.shape, BF16),
            pltpu.VMEM(pieces.shape, BF16),
            pltpu.SemaphoreType.DMA((frames.shape[0],)),
            pltpu.SemaphoreType.DMA((tiles,)),
        ],
        compiler_params=pltpu.CompilerParams(vmem_limit_bytes=VMEM_BYTES),
        name="pack",
    )(frames)


def mask_kernel(where_ref, out_ref):
    tile = where_ref[1]
    out_ref[...] = jnp.where(tile > 0, jnp.ones(out_ref.shape, F32), jnp.zeros(out_ref.shape, F32))


def odd_mask(where, channels):
    return pl.pallas_call(
        mask_kernel,
        in_specs=[pl.BlockSpec(memory_space=pltpu.SMEM)],
        out_specs=pl.BlockSpec(memory_space=pltpu.VMEM),
        out_shape=jax.ShapeDtypeStruct((8, channels), F32),
        name="odd_mask",
    )(where)


def silu(pre):
    return pre / (1.0 + jnp.exp(-pre))


def conv_kernel(
    rows, chunk, mask_hbm, y_hbm, w_hbm, odd_ref, even_ref,
    mask_ref, y_ref, w_ref, window_ref, y_sems, w_sem, mask_sem,
):
    channels = 2 * LANES
    loads = []
    for i, r in enumerate(range(0, rows, chunk)):
        part = pl.ds(r, chunk)
        loads.append(pltpu.make_async_copy(y_hbm.at[part], y_ref.at[part], y_sems.at[i]))
    weights = pltpu.make_async_copy(w_hbm, w_ref, w_sem)
    for load in loads:
        load.start()
    weights.start()
    mask = pltpu.make_async_copy(mask_hbm, mask_ref, mask_sem)
    mask.start()
    window_ref[0] = jnp.zeros(window_ref.shape[1:], BF16)
    window_ref[rows + 1] = jnp.zeros(window_ref.shape[1:], BF16)
    for f, act_ref in ((1, even_ref), (0, odd_ref)):
        for r in range(0, rows, chunk):
            if f == 1:
                loads[r // chunk].wait()
            place = lax.broadcasted_iota(jnp.int32, (chunk, COLS, LANES), 1)
            edges = y_ref[r : r + chunk, 4 * COLS :, :].astype(F32)
            for h in range(2):
                start = h * 2 * COLS + f * COLS
                main = y_ref[r : r + chunk, start : start + COLS, :]
                wide = main.astype(F32).reshape((chunk * COLS, LANES))
                row = h * 4 + f * 2
                shape = (chunk, COLS, LANES)
                earlier = pltpu.roll(wide, 1, 0).reshape(shape)
                later = pltpu.roll(wide, chunk * COLS - 1, 0).reshape(shape)
                earlier = jnp.where(place == 0, edges[:, row : row + 1], earlier)
                later = jnp.where(place == COLS - 1, edges[:, row + 1 : row + 2], later)
                for e, part in enumerate((earlier.astype(BF16), main, later.astype(BF16))):
                    lane = e * channels + h * LANES
                    window_ref[r + 1 : r + 1 + chunk, :, lane : lane + LANES] = part
        if f == 1:
            weights.wait()
            mask.wait()
            keep = mask_ref[0:1, :] > 0
        for r in range(0, rows, chunk):
            pre = jnp.zeros((chunk * COLS, channels), F32)
            for a in range(3):
                lhs = window_ref[r + a : r + a + chunk].reshape((chunk * COLS, 3 * channels))
                pre = pre + jnp.dot(lhs, w_ref[a], preferred_element_type=F32)
            value = silu(pre)
            if f == 0:
                value = jnp.where(keep, value, jnp.zeros_like(value))
            act_ref[r * COLS : (r + chunk) * COLS, :] = value.astype(BF16)


def spatial(mask, pieces, spatial_weight):
    rows = pieces.shape[0]
    channels = spatial_weight.shape[2]
    positions = rows * COLS
    chunk = 32
    weight = spatial_weight.reshape((3, 3 * channels, channels))
    hbm = pl.BlockSpec(memory_space=pltpu.HBM)
    vmem = pl.BlockSpec(memory_space=pltpu.VMEM)
    act = jax.ShapeDtypeStruct((positions, channels), BF16)
    return pl.pallas_call(
        functools.partial(conv_kernel, rows, chunk),
        in_specs=[hbm, hbm, hbm],
        out_specs=[vmem, vmem],
        out_shape=[act, act],
        scratch_shapes=[
            pltpu.VMEM(mask.shape, F32),
            pltpu.VMEM(pieces.shape, BF16),
            pltpu.VMEM(weight.shape, BF16),
            pltpu.VMEM((rows + 2, COLS, 3 * channels), BF16),
            pltpu.SemaphoreType.DMA((rows // chunk,)),
            pltpu.SemaphoreType.DMA,
            pltpu.SemaphoreType.DMA,
        ],
        compiler_params=pltpu.CompilerParams(vmem_limit_bytes=VMEM_BYTES),
        cost_estimate=pl.CostEstimate(
            flops=36 * positions * channels * channels,
            bytes_accessed=6_000_000,
            transcendentals=2 * positions * channels,
        ),
        name="spatial",
    )(mask, pieces, weight)


def outer_sum(act_ref, up_ref):
    return lax.dot_general(
        act_ref[...], up_ref[...], (((0,), (0,)), ((), ())), preferred_element_type=F32
    )


def late_taps_kernel(odd_ref, even_ref, u_hbm, grad_ref, u_ref, sem):
    load = pltpu.make_async_copy(u_hbm, u_ref, sem)
    load.start()
    channels = odd_ref.shape[1]
    blocks = u_ref.shape[1] // LANES
    first = channels // PIECE * blocks
    grad_ref[0, :first] = jnp.zeros((first, PIECE, LANES), F32)
    load.wait()
    for k, act_ref in ((1, odd_ref), (2, even_ref)):
        term = outer_sum(act_ref, u_ref)
        for g in range(channels // PIECE):
            half, group = divmod(k * channels + g * PIECE, 3 * channels // 2)
            for b in range(blocks):
                grad_ref[half, (group // PIECE) * blocks + b] = term[
                    g * PIECE : (g + 1) * PIECE, b * LANES : (b + 1) * LANES
                ]


def late_taps(odd, even, upstream):
    positions, channels = odd.shape
    out_channels = upstream.shape[1]
    count = 3 * channels * out_channels // (2 * PIECE * LANES)
    vmem = pl.BlockSpec(memory_space=pltpu.VMEM)
    return pl.pallas_call(
        late_taps_kernel,
        in_specs=[vmem, vmem, pl.BlockSpec(memory_space=pltpu.HBM)],
        out_specs=vmem,
        out_shape=jax.ShapeDtypeStruct((2, count, PIECE, LANES), F32),
        scratch_shapes=[pltpu.VMEM(upstream.shape, BF16), pltpu.SemaphoreType.DMA],
        compiler_params=pltpu.CompilerParams(vmem_limit_bytes=VMEM_BYTES),
        cost_estimate=pl.CostEstimate(
            flops=4 * positions * channels * out_channels,
            bytes_accessed=6_000_000,
            transcendentals=0,
        ),
        name="late_taps",
    )(odd, even, upstream)


def first_tap_kernel(where_ref, grad_ref, even_ref, next_hbm, mine_ref, sent_ref, next_ref, sem):
    load = pltpu.make_async_copy(next_hbm, next_ref, sem)
    load.start()
    side = where_ref[0]
    channels = even_ref.shape[1]
    blocks = next_ref.shape[1] // LANES
    first = channels // PIECE * blocks
    mine_ref[...] = grad_ref[side]
    sent_ref[...] = grad_ref[1 - side]
    load.wait()
    term = outer_sum(even_ref, next_ref)
    for p in range(first):
        g, b = divmod(p, blocks)
        part = term[g * PIECE : (g + 1) * PIECE, b * LANES : (b + 1) * LANES]
        mine_ref[p] = jnp.where(side == 0, part, mine_ref[p])
        sent_ref[p] = jnp.where(side == 0, sent_ref[p], part)


def first_tap(where, grad, even, following):
    positions, channels = even.shape
    out_channels = following.shape[1]
    vmem = pl.BlockSpec(memory_space=pltpu.VMEM)
    part = jax.ShapeDtypeStruct(grad.shape[1:], F32)
    return pl.pallas_call(
        first_tap_kernel,
        in_specs=[
            pl.BlockSpec(memory_space=pltpu.SMEM), vmem, vmem, pl.BlockSpec(memory_space=pltpu.HBM)
        ],
        out_specs=[vmem, vmem],
        out_shape=[part, part],
        scratch_shapes=[pltpu.VMEM(following.shape, BF16), pltpu.SemaphoreType.DMA],
        compiler_params=pltpu.CompilerParams(vmem_limit_bytes=VMEM_BYTES),
        cost_estimate=pl.CostEstimate(
            flops=2 * positions * channels * out_channels,
            bytes_accessed=6_000_000,
            transcendentals=0,
        ),
        name="first_tap",
    )(where, grad, even, following)


def latent_kernel(old_ref, odd_ref, even_ref, weight_ref, out_ref):
    total = jnp.dot(old_ref[...], weight_ref[0], preferred_element_type=F32)
    total = total + jnp.dot(odd_ref[...], weight_ref[1], preferred_element_type=F32)
    total = total + jnp.dot(even_ref[...], weight_ref[2], preferred_element_type=F32)
    out_ref[...] = total.astype(BF16)


def temporal(oldest, odd, even, temporal_weight):
    positions, channels = oldest.shape
    out_channels = temporal_weight.shape[2]
    step = 512
    tap = pl.BlockSpec((step, channels), lambda i: (i, 0))
    return pl.pallas_call(
        latent_kernel,
        grid=(positions // step,),
        in_specs=[
            tap,
            tap,
            tap,
            pl.BlockSpec(temporal_weight.shape, lambda i: (0, 0, 0)),
        ],
        out_specs=pl.BlockSpec((step, out_channels), lambda i: (i, 0)),
        out_shape=jax.ShapeDtypeStruct((positions, out_channels), BF16),
        compiler_params=pltpu.CompilerParams(vmem_limit_bytes=VMEM_BYTES),
        cost_estimate=pl.CostEstimate(
            flops=6 * positions * channels * out_channels,
            bytes_accessed=6_000_000,
            transcendentals=0,
        ),
        name="temporal",
    )(oldest, odd, even, temporal_weight)


def pair_kernel(mine_ref, away_ref, out_ref):
    count = mine_ref.shape[0]
    out_ref[:count] = (mine_ref[...] + away_ref[...]).astype(BF16)
    out_ref[count:] = jnp.zeros((out_ref.shape[0] - count, *out_ref.shape[1:]), BF16)


def pair_sum(mine, away, devices):
    vmem = pl.BlockSpec(memory_space=pltpu.VMEM)
    return pl.pallas_call(
        pair_kernel,
        in_specs=[vmem, vmem],
        out_specs=vmem,
        out_shape=jax.ShapeDtypeStruct((devices, *mine.shape[1:]), BF16),
        compiler_params=pltpu.CompilerParams(vmem_limit_bytes=VMEM_BYTES),
        name="pair_sum",
    )(mine, away)


def total_kernel(parts_ref, out_ref):
    total = jnp.sum(parts_ref[...].astype(F32), axis=0).astype(BF16)
    out_ref[...] = jnp.broadcast_to(total[None], out_ref.shape)


def total_for_all(parts):
    vmem = pl.BlockSpec(memory_space=pltpu.VMEM)
    return pl.pallas_call(
        total_kernel,
        in_specs=[vmem],
        out_specs=vmem,
        out_shape=jax.ShapeDtypeStruct(parts.shape, BF16),
        compiler_params=pltpu.CompilerParams(vmem_limit_bytes=VMEM_BYTES),
        name="total_for_all",
    )(parts)


def unpack_kernel(where_ref, own_ref, away_ref, out_ref):
    side = where_ref[0]
    blocks = out_ref.shape[2] // LANES
    for ref, half in ((own_ref, side), (away_ref, 1 - side)):
        for p in range(out_ref.shape[1] // PIECE * blocks):
            g, b = divmod(p, blocks)
            out_ref[half, g * PIECE : (g + 1) * PIECE, b * LANES : (b + 1) * LANES] = ref[p].astype(F32)


def unpack(where, own, away, height, width):
    vmem = pl.BlockSpec(memory_space=pltpu.VMEM)
    return pl.pallas_call(
        unpack_kernel,
        in_specs=[pl.BlockSpec(memory_space=pltpu.SMEM), vmem, vmem],
        out_specs=vmem,
        out_shape=jax.ShapeDtypeStruct((2, height // 2, width), F32),
        compiler_params=pltpu.CompilerParams(vmem_limit_bytes=VMEM_BYTES),
        name="unpack",
    )(where, own, away)


def body(video, spatial_weight, temporal_weight, latent_grad):
    tiles, chans = lax.axis_size("tile"), lax.axis_size("chan")
    devices = tiles * chans
    where = jnp.stack([lax.axis_index("segment"), lax.axis_index("tile")]).astype(jnp.int32)
    out_channels = latent_grad.shape[4]
    upstream = other_core(latent_grad)
    shift = [
        (s * tiles + j, (1 - s) * tiles + j - 1) for s in range(2) for j in range(1, tiles)
    ]
    following = lax.ppermute(latent_grad, ("segment", "tile"), shift)
    frames = pltpu.with_memory_space_constraint(video[0, :, 0], pltpu.HBM)
    pieces = pltpu.with_memory_space_constraint(exchange(pack(frames, tiles, chans)), pltpu.HBM)
    mask = pltpu.with_memory_space_constraint(odd_mask(where, video.shape[4]), pltpu.HBM)
    odd, even = spatial(mask, pieces, spatial_weight)
    later = late_taps(odd, even, upstream.reshape((-1, out_channels)))
    mine, sent = first_tap(where, later, even, following.reshape((-1, out_channels)))
    oldest = lax.ppermute(even, "tile", [(i, i + 1) for i in range(tiles - 1)])
    pair = pair_sum(mine, other_core(sent), devices)
    whole = exchange(total_for_all(exchange(pair)))
    latents = temporal(oldest, odd, even, temporal_weight).reshape(upstream.shape)
    whole, latents = lax.optimization_barrier((whole, latents))
    height = temporal_weight.shape[0] * temporal_weight.shape[1]
    grad = unpack(where, whole, other_core(whole), height, out_channels)
    return (latents, grad.reshape(temporal_weight.shape))


def solution(mesh):
    placed = (
        P("segment", None, ("tile", "chan"), None, None),
        P(),
        P(),
        P("segment", "tile", None, "chan", None),
    )
    return jax.shard_map(
        body,
        mesh=mesh,
        in_specs=placed,
        out_specs=(P("segment", "tile", None, "chan", None), P()),
        check_vma=False,
    )
```
